32 devices in a mesh: groups: 2 (over x), slab: 8 (over z, y), chan: 2 (over core).
Axes of the slice: x: 2, y: 2, z: 4, core: 2. Of those that a mesh axis runs over, the one named last changes fastest.
Arguments:
- point_features: bfloat16 [1024, 64, 128], P(('groups', 'slab'), 'chan'), parts along dimension 0, may hold values from -6 to 6
- kernel_blocks: bfloat16 [1024, 128, 128], P(('groups', 'slab')), parts along dimension 0, may hold values from -0.5 to 0.5
- owner_slab: int32 [1024, 1], P(('groups', 'slab')), parts along dimension 0, may hold values from 0 to 7; in each aligned block of 64 rows (0 to 63, 64 to 127, ...) at most 16 rows name the same one
- tile_index: int32 [1024], P(('groups', 'slab')), parts along dimension 0, may hold values from 0 to 255
- point_count: int32 [1024], P(('groups', 'slab')), parts along dimension 0, may hold values from 32 to 128
- targets: float32 [1024, 4, 128], P(('groups', 'slab')), parts along dimension 0, may hold values from -6 to 6
- w_lift: bfloat16 [64, 64], replicated, may hold values from -0.75 to 0.75
- w_conv: bfloat16 [27, 64, 64], P(None, None, 'chan'), may hold values from -0.15625 to 0.15625
- w_out: bfloat16 [4, 64], P(None, 'chan'), may hold values from -0.75 to 0.75
Outputs:
- grad_conv: float32 [54, 64, 64], P('groups', None, 'chan'), parts along dimension 0
- grad_out: float32 [8, 64], P('groups', 'chan'), parts along dimension 0
- mean_error: float32 [2], P('groups'), parts along dimension 0
The draws below stay inside these ranges and needn't reach their ends.
There are 2 independent parts, one for each index of `groups`. The reference program is written for one: setup_inputs(seed, part) draws one part's arguments, and reference() takes and returns one part's arrays. A program takes and returns all parts, laid end to end along the dimension named above; an argument that names none is the same for every part. Nothing has to cross between parts.
Inputs may be any that keep to these rules, and one draw needn't show every extreme that they name: `owner_slab`: among the 64 blocks of one device at most 16 name the same slab, a bound that some block reaches of them.
All inputs are finite; a program needn't handle non-finite values.
Results may differ from the reference program's by a relative error of at most 0.00099.
Values may be sent and summed in bfloat16 or wider, within the bound.
A program may use at most 512 MiB of HBM per device.

```python
import math
import jax
import jax.numpy as jnp
import numpy as np
from jax import lax

F = 64
C = 64
OUT = 4
B = 128
GY = 128
GX = 32
NB = 64
CAP = 16
NT = 256
NZ = 64
NBLK = 512
N_SLAB = 8


def place_ends(array, own_key, least, top_value):
    index_at = [jax.random.randint(jax.random.fold_in(own_key, axis), (), 0, length) for axis, length in enumerate(array.shape)]
    main_axis = array.shape.index(max(array.shape))
    next_to = index_at[:main_axis] + [(index_at[main_axis] + 1) % array.shape[main_axis]] + index_at[main_axis + 1:]
    return array.at[tuple(index_at)].set(least).at[tuple(next_to)].set(top_value)


def block_scale(key, extent, cuts, least, top_value):
    def one(dim, parts):
        steps = jax.random.uniform(jax.random.fold_in(jax.random.fold_in(key, 6), dim), (parts,), jnp.float32, least / len(cuts), top_value / len(cuts))
        return jnp.repeat(jnp.exp(steps), extent[dim] // parts).reshape((-1,) + (1,) * (len(extent) - dim - 1))

    factor_of = one(*cuts[0])
    for cut in cuts[1:]:
        factor_of = factor_of * one(*cut)
    return factor_of


def routed_block(own_key, own, number, rows, number_of, top, bound, skew):
    ranking = jax.random.permutation(own_key, number_of)
    packed, usual = portions_of(number_of, rows * top, bound, skew, True), portions_of(number_of, rows * top, bound, skew, False)
    places = jnp.arange(number_of)

    def named(sizes, rotation):
        used = int((sizes > 0).sum())
        fixed = max(1, used // 4)
        shifted = fixed + (places - fixed + rotation * (used - fixed)) % max(1, number_of - fixed)
        return jnp.zeros((number_of,), jnp.int32).at[ranking[jnp.where(places < fixed, places, shifted)]].set(jnp.asarray(sizes, jnp.int32))

    sizes = jnp.where(number % 4 == 0, named(packed, number // 4), named(usual, number - number // 4 - 1))
    mixed = jax.random.permutation(jax.random.fold_in(own, 3), number_of)
    giver, sink = mixed[0:number_of // 2 * 2:2], mixed[1:number_of // 2 * 2:2]
    room = jnp.minimum(sizes[giver] - 1, bound - sizes[sink]) // 2
    room = jnp.where((giver == ranking[0]) | (sink == ranking[0]) | (sizes[sink] == 0), 0, jnp.maximum(room, 0))
    shifted = jax.random.randint(jax.random.fold_in(own, 4), (number_of // 2,), 0, 1 << 20) % (room + 1)
    sizes = sizes.at[giver].add(-shifted).at[sink].add(shifted)
    items = jnp.searchsorted(jnp.cumsum(sizes), jnp.arange(rows * top), side="right").astype(jnp.int32)
    listing = items.reshape(top, rows).T
    listing = listing[jax.random.permutation(jax.random.fold_in(own, 1), rows)]
    rotation = jax.random.randint(jax.random.fold_in(own, 2), (rows, 1), 0, top)
    return jnp.take_along_axis(listing, (jnp.arange(top)[None, :] + rotation) % top, axis=1)


def portions_of(number_of, total, reach, lean, full):
    weights = [(1 << 20) // math.isqrt(rank ** lean) + 1 for rank in range(1, number_of + 1)]
    largest = reach if full else min(reach, max(-(-total // number_of), total * weights[0] // sum(weights)))
    least = 1 if total - largest >= number_of - 1 else 0
    given, spare = [largest] + [least] * (number_of - 1), total - largest - least * (number_of - 1)
    while spare > 0:
        free = [i for i in range(1, number_of) if given[i] < largest] or [i for i in range(1, number_of) if given[i] < reach]
        mass, left = sum([weights[i] for i in free]), spare
        for i in free:
            more = min(reach - given[i], max(1, left * weights[i] // mass), spare)
            given[i] = given[i] + more
            spare = spare - more
    return np.array(given)


def gaussian(stream_key, shape, scale, reach, pieces=(), kind=jnp.bfloat16):
    array = jax.random.normal(stream_key, shape, jnp.float32) * scale
    if len(pieces) > 0:
        array = block_scale(stream_key, shape, pieces, -0.22, 0.18) * array
    return jnp.clip(array, min=-reach, max=reach).astype(kind)


def setup_inputs(seed: int = 0, part: int = 0) -> dict:
    key_of = jax.random.split(jax.random.key(seed), 10)
    own_keys = jax.random.split(jax.random.fold_in(key_of[9], part), 10)
    point_features = gaussian(own_keys[0], (NBLK, F, B), 1.0, 6.0, ((0, 8), (1, 2)))
    kernel_blocks = gaussian(own_keys[1], (NBLK, B, GY), B ** -0.5, 0.5, ((0, 8),))
    owner_slab_keys = jax.random.split(jax.random.fold_in(own_keys[2], 1), NBLK // NB)
    owner_slab_turns = jax.random.permutation(jax.random.fold_in(own_keys[2], 3), NBLK // NB)
    owner_slab = jax.vmap(lambda own, number: routed_block(jax.random.fold_in(own_keys[2], 2), own, number, NB, N_SLAB, 1, CAP, 2))(owner_slab_keys, owner_slab_turns).reshape((NBLK, 1))
    tile_index = place_ends(jax.random.randint(own_keys[3], (NBLK,), 0, NT), jax.random.fold_in(own_keys[3], 1), 0, NT - 1).astype(jnp.int32)
    point_count = place_ends(jax.random.randint(own_keys[4], (NBLK,), B // 4, B + 1), jax.random.fold_in(own_keys[4], 1), B // 4, B).astype(jnp.int32)
    targets = gaussian(own_keys[5], (NBLK, OUT, B), 1.0, 6.0, ((0, 8),), jnp.float32)
    w_lift = gaussian(key_of[6], (F, C), F ** -0.5, 0.75)
    w_conv = gaussian(key_of[7], (27, C, C), (27 * C) ** -0.5, 0.15625, ((2, 2),))
    w_out = gaussian(key_of[8], (OUT, C), C ** -0.5, 0.75, ((1, 2),))
    return {"point_features": point_features, "kernel_blocks": kernel_blocks, "owner_slab": owner_slab, "tile_index": tile_index, "point_count": point_count, "targets": targets, "w_lift": w_lift, "w_conv": w_conv, "w_out": w_out}


HIGH = lax.Precision.HIGHEST

def reference(point_features, kernel_blocks, owner_slab, tile_index, point_count, targets, w_lift, w_conv, w_out):
    live_mask = jnp.arange(B, dtype=jnp.int32)[None, :] < point_count[:, None]
    masked = jnp.where(live_mask[:, None, :], point_features.astype(jnp.float32), 0.0)
    kernel_f = kernel_blocks.astype(jnp.float32)
    lifted = jnp.einsum('kfb,kbv->kfv', masked, kernel_f, precision=HIGH).astype(jnp.bfloat16)
    place = (owner_slab[:, 0] * NT + tile_index).astype(jnp.int32)
    surface = jnp.zeros((N_SLAB * NT, F, GY), jnp.float32).at[place].add(lifted.astype(jnp.float32))
    surface = surface.astype(jnp.bfloat16).astype(jnp.float32)
    latent = jnp.einsum('fc,tfv->ctv', w_lift.astype(jnp.float32), surface, precision=HIGH).astype(jnp.bfloat16)
    volume = latent.reshape(C, NZ, GX, GY).astype(jnp.float32)
    weights = w_conv.astype(jnp.float32).reshape(3, 3, 3, C, C).transpose(4, 3, 0, 1, 2)

    def convolve(kern):
        return lax.conv_general_dilated(volume[None], kern, (1, 1, 1), ((1, 1), (1, 1), (1, 1)), dimension_numbers=('NCDHW', 'OIDHW', 'NCDHW'), precision=HIGH)[0]
    hidden, pullback = jax.vjp(convolve, weights)
    mixed = (volume + jax.nn.silu(hidden)).astype(jnp.bfloat16)
    mixed_flat = mixed.reshape(C, N_SLAB * NT, GY).astype(jnp.float32)
    tile_rows = jnp.take(mixed_flat, place, axis=1)
    at_points = jnp.einsum('ckv,kbv->kcb', tile_rows, kernel_f, precision=HIGH)
    w_out_f = w_out.astype(jnp.float32)
    prediction = jnp.einsum('oc,kcb->kob', w_out_f, at_points, precision=HIGH)
    error = jnp.where(live_mask[:, None, :], prediction - targets, 0.0)
    doubled = (2.0 * error).astype(jnp.bfloat16)
    doubled = lax.optimization_barrier(doubled).astype(jnp.float32)
    residue = jnp.einsum('kob,kbv->kov', doubled, kernel_f, precision=HIGH)
    head_grads = jnp.einsum('kob,kcb->oc', doubled, at_points, precision=HIGH)
    block_grads = jnp.einsum('oc,kov->kcv', w_out_f, residue, precision=HIGH)
    mixed_grads = jnp.zeros((N_SLAB * NT, C, GY), jnp.float32).at[place].add(block_grads)
    mixed_grads = mixed_grads.transpose(1, 0, 2).reshape(C, NZ, GX, GY)
    sigmoid_h = jax.nn.sigmoid(hidden)
    hidden_grads = (mixed_grads * sigmoid_h * (1.0 + hidden * (1.0 - sigmoid_h))).astype(jnp.bfloat16)
    hidden_grads = lax.optimization_barrier(hidden_grads).astype(jnp.float32)
    kernel_grads, = pullback(hidden_grads)
    conv_grads = kernel_grads.transpose(2, 3, 4, 1, 0).reshape(27, C, C)
    total = jnp.sum(point_count).astype(jnp.float32)
    factor = lax.rsqrt(OUT * total)
    mean_error = (jnp.sum(error * error) / (OUT * total)).reshape(1)
    return (conv_grads * factor, head_grads * factor, mean_error)
```

```python
import jax
import jax.numpy as jnp
from jax import lax
from jax.experimental import pallas as pl
from jax.experimental.pallas import tpu as pltpu
from jax.sharding import PartitionSpec as P

GX = 32
CZ = 8


HIGH = lax.Precision.HIGHEST
VMEM_BYTES = 56 * 1024 * 1024
VMEM = pl.BlockSpec(memory_space=pltpu.VMEM)


def lift_kernel(sel_ref, own_ref, peer_ref, w_ref, out_ref, surf_ref):
    tiles, feats, width = out_ref.shape[0], w_ref.shape[1], out_ref.shape[2]
    half = feats // 2
    sel = sel_ref[...]
    for side, ref in enumerate((own_ref, peer_ref)):
        for pair in range(half // 2):
            part = jnp.dot(
                sel,
                ref[:, 2 * pair * width : 2 * (pair + 1) * width],
                preferred_element_type=jnp.float32,
            )
            for j in range(2):
                feat = side * half + 2 * pair + j
                surf_ref[pl.ds(feat, tiles, stride=feats), :] = part[:, j * width : (j + 1) * width]
    w = w_ref[...]

    def body(i, carry):
        rows = surf_ref[pl.ds(pl.multiple_of(i * 2 * feats, 2 * feats), 2 * feats), :]
        rows = rows.astype(jnp.bfloat16)
        both = jnp.concatenate([rows[:feats], rows[feats:]], axis=1)
        res = jnp.dot(w, both, preferred_element_type=jnp.float32).astype(jnp.bfloat16)
        out_ref[2 * i] = res[:, :width]
        out_ref[2 * i + 1] = res[:, width:]
        return carry

    lax.fori_loop(0, tiles // 2, body, 0, unroll=4)


def shifts(array):
    width = array.shape[1]
    lane = lax.broadcasted_iota(jnp.int32, array.shape, 1)
    right = jnp.where(lane == 0, 0.0, pltpu.roll(array, 1, 1))
    left = jnp.where(lane == width - 1, 0.0, pltpu.roll(array, width - 1, 1))
    return right, left


def patch_of(ext_ref, z, x, number):
    rows = []
    for a in range(3):
        for e in range(3):
            rows.append(
                jnp.concatenate([ext_ref[z + a, x + e + j] for j in range(number)], axis=1)
            )
    return jnp.concatenate(rows, axis=0)


def conv_kernel(lat_ref, low_ref, high_ref, w_ref, wo_ref, ext_ref, hidden_ref, mixed_ref, p_ref):
    planes, _, channels, width = ext_ref.shape
    half = hidden_ref.shape[1]
    components = p_ref.shape[1]
    zero = jnp.zeros((channels, width), ext_ref.dtype)
    for z in range(planes):
        ext_ref[z, 0] = zero
        ext_ref[z, GX + 1] = zero

    def fill(x, carry):
        ext_ref[0, x + 1] = low_ref[x]
        ext_ref[planes - 1, x + 1] = high_ref[x]
        for z in range(planes - 2):
            ext_ref[z + 1, x + 1] = lat_ref[z * GX + x]
        return carry

    lax.fori_loop(0, GX, fill, 0)
    w = w_ref[...]
    wo = wo_ref[...]

    def body(i, carry):
        z = i // (GX // 2)
        x = (i % (GX // 2)) * 2
        res = jnp.dot(w, patch_of(ext_ref, z, x, 2), preferred_element_type=jnp.float32)
        both = []
        for j in range(2):
            t = z * GX + x + j
            part = res[:, j * width : (j + 1) * width]
            right, _ = shifts(part[:half])
            _, left = shifts(part[2 * half :])
            hidden = part[half : 2 * half] + right + left
            own = ext_ref[z + 1, x + 1 + j][:half].astype(jnp.float32)
            mixed = (own + hidden * (1.0 / (1.0 + jnp.exp(-hidden)))).astype(jnp.bfloat16)
            hidden_ref[t] = hidden
            mixed_ref[t] = mixed
            both.append(mixed)
        heads = jnp.dot(wo, jnp.concatenate(both, axis=1), preferred_element_type=jnp.float32)
        for j in range(2):
            p_ref[z * GX + x + j] = heads[:components, j * width : (j + 1) * width]
        return carry

    lax.fori_loop(0, (planes - 2) * GX // 2, body, 0, unroll=2)


def grad_kernel(ext_ref, hidden_ref, mixed_ref, r_ref, wo_ref, grad_ref, head_ref):
    planes, _, _, width = ext_ref.shape
    components = r_ref.shape[1]
    number = 4
    grad_ref[...] = jnp.zeros_like(grad_ref)
    head_ref[...] = jnp.zeros_like(head_ref)

    def body(i, carry):
        z = i // (GX // number)
        x = (i % (GX // number)) * number
        columns = []
        heads = [head_ref[o] for o in range(components)]
        for j in range(number):
            t = z * GX + x + j
            hidden = hidden_ref[t]
            mixed = mixed_ref[t].astype(jnp.float32)
            res = r_ref[t]
            total = None
            for o in range(components):
                row = res[o : o + 1]
                term = wo_ref[o] * row
                total = term if total is None else total + term
                heads[o] = heads[o] + mixed * row
            s = 1.0 / (1.0 + jnp.exp(-hidden))
            grads = total * s * (1.0 + hidden * (1.0 - s))
            right, left = shifts(grads)
            columns.append(jnp.concatenate([left, grads, right], axis=0).astype(jnp.bfloat16))
        for o in range(components):
            head_ref[o] = heads[o]
        grad_ref[...] += lax.dot_general(
            patch_of(ext_ref, z, x, number),
            jnp.concatenate(columns, axis=1),
            (((1,), (1,)), ((), ())),
            preferred_element_type=jnp.float32,
        )
        return carry

    lax.fori_loop(0, (planes - 2) * GX // number, body, 0)


def call(kernel, shapes, number, flops, scratch=()):
    return pl.pallas_call(
        kernel,
        out_shape=shapes,
        in_specs=[VMEM] * number,
        out_specs=jax.tree.map(lambda _: VMEM, shapes),
        scratch_shapes=list(scratch),
        compiler_params=pltpu.CompilerParams(vmem_limit_bytes=VMEM_BYTES),
        cost_estimate=pl.CostEstimate(
            flops=flops, bytes_accessed=1 << 23, transcendentals=1 << 20
        ),
    )


def swapped_halves(array, axis, flag):
    half = array.shape[axis] // 2
    first = lax.slice_in_dim(array, 0, half, axis=axis)
    second = lax.slice_in_dim(array, half, 2 * half, axis=axis)
    return jnp.where(flag == 0, array, jnp.concatenate([second, first], axis=axis))


def exchanged(array):
    return lax.ppermute(array, "chan", [(0, 1), (1, 0)])


def to_all(array):
    return lax.all_to_all(array, "slab", split_axis=0, concat_axis=0, tiled=True)


def per_device(
    point_features,
    kernel_blocks,
    owner_slab,
    tile_index,
    point_count,
    targets,
    w_lift,
    w_conv,
    w_out,
):
    owners = lax.axis_size("slab")
    blocks = point_features.shape[0]
    half_feat = point_features.shape[1]
    points = point_features.shape[2]
    width = kernel_blocks.shape[2]
    channels = w_lift.shape[1]
    half_chan = w_conv.shape[2]
    components = targets.shape[1]
    capacity = max(2, 2 * blocks // owners)
    slots = owners * capacity
    tiles = CZ * GX
    chan_lane = lax.axis_index("chan")
    f32, bf16 = jnp.float32, jnp.bfloat16

    w_up = swapped_halves(swapped_halves(w_lift, 0, chan_lane), 1, chan_lane).T
    w_taps = swapped_halves(w_conv, 1, chan_lane).reshape(3, 3, 3, channels, half_chan)
    w_taps = w_taps.transpose(2, 4, 0, 1, 3).reshape(3 * half_chan, 9 * channels)
    w_head = jnp.pad(w_out, ((0, 16 - components), (0, 0)))
    w_spread = jnp.broadcast_to(w_out.astype(f32)[:, :, None], (components, half_chan, width))

    live_mask = lax.broadcasted_iota(jnp.int32, (blocks, points), 1) < point_count[:, None]
    masked = jnp.where(live_mask[:, None, :], point_features, jnp.zeros_like(point_features))
    lifted = jnp.einsum("kfb,kbv->kfv", masked, kernel_blocks, preferred_element_type=f32)
    lifted = lifted.astype(bf16)
    target_owner = owner_slab[:, 0]
    matches = (target_owner[:, None] == jnp.arange(owners, dtype=jnp.int32)[None, :]).astype(
        jnp.int32
    )
    earlier = jnp.cumsum(matches, axis=0) - matches
    position = target_owner * capacity + jnp.sum(earlier * matches, axis=1)
    placing = position[None, :] == jnp.arange(slots, dtype=jnp.int32)[:, None]
    place_b = placing.astype(bf16)
    place_f = placing.astype(f32)
    outgoing = jnp.einsum(
        "sk,kn->sn",
        place_b,
        lifted.reshape(blocks, half_feat * width),
        preferred_element_type=f32,
    ).astype(bf16)
    tile_ids = (jnp.sum(jnp.where(placing, tile_index[None, :] + 1, 0), axis=1) - 1).astype(bf16)
    id_lanes = jnp.broadcast_to(tile_ids[:, None], (slots, 128))
    packed = jnp.concatenate([outgoing, id_lanes], axis=1)
    arrived = to_all(packed.reshape(owners, capacity, -1)).reshape(slots, -1)
    own_slots = arrived[:, : half_feat * width]
    peer_slots = exchanged(own_slots)
    arrived_ids = arrived[:, half_feat * width].astype(f32).astype(jnp.int32)
    selecting = arrived_ids[None, :] == jnp.arange(tiles, dtype=jnp.int32)[:, None]
    select_f = selecting.astype(f32)

    latent = call(
        lift_kernel,
        jax.ShapeDtypeStruct((tiles, channels, width), bf16),
        4,
        1 << 30,
        [pltpu.VMEM((tiles * channels, width), f32)],
    )(selecting.astype(bf16), own_slots, peer_slots, w_up)

    up = [(i, i + 1) for i in range(owners - 1)]
    down = [(j, i) for i, j in up]
    before = lax.ppermute(latent[tiles - GX :], "slab", up)
    after = lax.ppermute(latent[:GX], "slab", down)
    extended, hidden, mixed, heads = call(
        conv_kernel,
        (
            jax.ShapeDtypeStruct((CZ + 2, GX + 2, channels, width), bf16),
            jax.ShapeDtypeStruct((tiles, half_chan, width), f32),
            jax.ShapeDtypeStruct((tiles, half_chan, width), bf16),
            jax.ShapeDtypeStruct((tiles, components, width), f32),
        ),
        5,
        1 << 32,
    )(latent, before, after, w_taps, w_head)

    returning = jnp.einsum(
        "ts,tn->sn", select_f, heads.reshape(tiles, components * width), precision=HIGH
    )
    received = to_all(returning.reshape(owners, capacity, -1)).reshape(slots, -1)
    per_block = jnp.einsum("sk,sn->kn", place_f, received, precision=HIGH)
    per_block = (per_block + exchanged(per_block)).reshape(blocks, components, width)
    first = lax.reduce_precision(per_block, 8, 7)
    second = lax.reduce_precision(per_block - first, 8, 7)
    third = per_block - first - second
    pieces = jnp.concatenate([first, second, third], axis=1).astype(bf16)
    terms = jnp.einsum("kqv,kbv->kqb", pieces, kernel_blocks, preferred_element_type=f32)
    terms = terms.reshape(blocks, 3, components, points)
    prediction = terms[:, 0] + (terms[:, 1] + terms[:, 2])
    error = jnp.where(live_mask[:, None, :], prediction - targets, 0.0)
    doubled = (2.0 * error).astype(bf16)
    residue = jnp.einsum("kob,kbv->kov", doubled, kernel_blocks, preferred_element_type=f32)
    sent = jnp.einsum(
        "sk,kn->sn", place_f, residue.reshape(blocks, components * width), precision=HIGH
    )
    slot_residue = to_all(sent.reshape(owners, capacity, -1)).reshape(slots, -1)
    tile_residue = jnp.einsum("ts,sn->tn", select_f, slot_residue, precision=HIGH)

    conv_terms, head_terms = call(
        grad_kernel,
        (
            jax.ShapeDtypeStruct((9 * channels, 3 * half_chan), f32),
            jax.ShapeDtypeStruct((components, half_chan, width), f32),
        ),
        5,
        1 << 32,
    )(extended, hidden, mixed, tile_residue.reshape(tiles, components, width), w_spread)

    squared = jnp.sum(error * error)
    point_total = jnp.sum(point_count).astype(f32)
    sizes = (conv_terms.size, components * half_chan)
    flat = jnp.concatenate(
        [
            conv_terms.reshape(-1),
            jnp.sum(head_terms, axis=2).reshape(-1),
            squared.reshape(1),
            point_total.reshape(1),
        ]
    )
    piece = -(-flat.shape[0] // (owners * 128)) * 128
    flat = jnp.pad(flat, (0, owners * piece - flat.shape[0])).reshape(owners, piece)
    share = jnp.sum(to_all(flat), axis=0)
    summed = to_all(jnp.broadcast_to(share[None], (owners, piece))).reshape(-1)
    conv_sum = summed[: sizes[0]].reshape(3, 3, channels, 3, half_chan)
    conv_sum = conv_sum.transpose(0, 1, 3, 2, 4).reshape(27, channels, half_chan)
    conv_sum = swapped_halves(conv_sum, 1, chan_lane)
    head_sum = summed[sizes[0] : sizes[0] + sizes[1]].reshape(components, half_chan)
    error_sum = summed[sizes[0] + sizes[1]]
    total_sum = summed[sizes[0] + sizes[1] + 1]
    factor = lax.rsqrt(components * total_sum)
    return (conv_sum * factor, head_sum * factor, (error_sum / (components * total_sum)).reshape(1))


def solution(mesh):
    placed = (
        P(("groups", "slab"), "chan", None),
        P(("groups", "slab"), None, None),
        P(("groups", "slab"), None),
        P(("groups", "slab")),
        P(("groups", "slab")),
        P(("groups", "slab"), None, None),
        P(),
        P(None, None, "chan"),
        P(None, "chan"),
    )
    return jax.shard_map(
        per_device,
        mesh=mesh,
        in_specs=placed,
        out_specs=(P("groups", None, "chan"), P("groups", "chan"), P("groups")),
        check_vma=False,
    )
```

```python
import jax
import jax.numpy as jnp
from jax import lax
from jax.experimental import pallas as pl
from jax.experimental.pallas import tpu as pltpu
from jax.sharding import PartitionSpec as P

GX = 32
CZ = 8


HIGH = lax.Precision.HIGHEST
VMEM_BYTES = 56 * 1024 * 1024
VMEM = pl.BlockSpec(memory_space=pltpu.VMEM)


def lift_kernel(sel_ref, own_ref, peer_ref, w_ref, out_ref, surf_ref):
    width, feats = out_ref.shape[3], w_ref.shape[1]
    tiles = sel_ref.shape[0]
    half = feats // 2
    zero = jnp.zeros(out_ref.shape[2:], out_ref.dtype)
    for z in range(out_ref.shape[0]):
        out_ref[z, 0] = zero
        out_ref[z, GX + 1] = zero
    sel = sel_ref[...]
    for side, ref in enumerate((own_ref, peer_ref)):
        for pair in range(half // 2):
            part = jnp.dot(
                sel,
                ref[:, 2 * pair * width : 2 * (pair + 1) * width],
                preferred_element_type=jnp.float32,
            )
            for j in range(2):
                feat = side * half + 2 * pair + j
                surf_ref[pl.ds(feat, tiles, stride=feats), :] = part[:, j * width : (j + 1) * width]
    w = w_ref[...]

    def body(i, carry):
        rows = surf_ref[pl.ds(pl.multiple_of(i * 2 * feats, 2 * feats), 2 * feats), :]
        rows = rows.astype(jnp.bfloat16)
        both = jnp.concatenate([rows[:feats], rows[feats:]], axis=1)
        res = jnp.dot(w, both, preferred_element_type=jnp.float32).astype(jnp.bfloat16)
        z = i // (GX // 2)
        x = (i % (GX // 2)) * 2
        out_ref[z, x + 1] = res[:, :width]
        out_ref[z, x + 2] = res[:, width:]
        return carry

    lax.fori_loop(0, tiles // 2, body, 0, unroll=4)


def shifted(array, by):
    width = array.shape[1]
    lane = lax.broadcasted_iota(jnp.int32, array.shape, 1)
    edge = 0 if by == 1 else width - 1
    return jnp.where(lane == edge, 0.0, pltpu.roll(array, by % width, 1))


def patch_of(planes, x, number):
    rows = []
    for ref, z in planes:
        for e in range(3):
            rows.append(jnp.concatenate([ref[z, x + e + j] for j in range(number)], axis=1))
    return jnp.concatenate(rows, axis=0)


def conv_pairs(pairs, w_ref, wo_ref, slope_ref, mixed_ref, p_ref):
    half, width = slope_ref.shape[1:]
    components = p_ref.shape[0] // slope_ref.shape[0]
    w = w_ref[...]
    wo = wo_ref[...]
    for number, planes in enumerate(pairs):

        def body(i, carry, number=number, planes=planes):
            x = i * 2
            res = jnp.dot(w, patch_of(planes, x, 2), preferred_element_type=jnp.float32)
            tiles = []
            for d in range(2):
                ref, z = planes[d + 1]
                for j in range(2):
                    t = (2 * number + d) * GX + x + j
                    part = res[3 * half * d : 3 * half * (d + 1), j * width : (j + 1) * width]
                    hidden = part[half : 2 * half] + (
                        shifted(part[:half], 1) + shifted(part[2 * half :], -1)
                    )
                    s = 1.0 / (1.0 + jnp.exp(-hidden))
                    own = ref[z, x + 1 + j][:half].astype(jnp.float32)
                    mixed = (own + hidden * s).astype(jnp.bfloat16)
                    slope_ref[t] = s * (1.0 + hidden * (1.0 - s))
                    mixed_ref[t] = mixed
                    tiles.append(mixed)
            heads = jnp.dot(
                wo, jnp.concatenate(tiles, axis=0), preferred_element_type=jnp.float32
            )
            rows = 2 * components
            for d in range(2):
                start = pl.multiple_of(((2 * number + d) * GX + x) * components, rows)
                p_ref[pl.ds(start, rows), :] = heads[d * rows : (d + 1) * rows]
            return carry

        lax.fori_loop(0, GX // 2, body, 0, unroll=2)


def inner_kernel(lat_ref, w_ref, wo_ref, slope_ref, mixed_ref, p_ref):
    pairs = [[(lat_ref, z + k) for k in range(-1, 3)] for z in range(2, CZ - 2, 2)]
    conv_pairs(pairs, w_ref, wo_ref, slope_ref, mixed_ref, p_ref)


def outer_kernel(lat_ref, low_ref, high_ref, w_ref, wo_ref, slope_ref, mixed_ref, p_ref):
    pairs = outer_pairs(lat_ref, low_ref, high_ref)
    conv_pairs(pairs, w_ref, wo_ref, slope_ref, mixed_ref, p_ref)


def outer_pairs(lat_ref, low_ref, high_ref):
    first = [(low_ref, 0)] + [(lat_ref, z) for z in range(3)]
    return [first, [(lat_ref, z) for z in range(CZ - 3, CZ)] + [(high_ref, 0)]]


def grad_kernel(
    lat_ref, low_ref, high_ref, inner_slope, inner_mixed, outer_slope, outer_mixed,
    r_ref, wo_ref, grad_ref, head_ref, acc_ref,
):
    width = lat_ref.shape[3]
    components, half = head_ref.shape[:2]
    number = 8
    acc_ref[...] = jnp.zeros_like(acc_ref)
    head_ref[...] = jnp.zeros_like(head_ref)
    ends = outer_pairs(lat_ref, low_ref, high_ref)
    work = [(0, ends[0], outer_slope, outer_mixed, 0)]
    for z in range(2, CZ - 2, 2):
        planes = [(lat_ref, z + k) for k in range(-1, 3)]
        work.append((z, planes, inner_slope, inner_mixed, z - 2))
    work.append((CZ - 2, ends[1], outer_slope, outer_mixed, 2))
    rest = jnp.zeros((128 - 3 * half, width), jnp.float32)
    for z, planes, slope_ref, mixed_ref, held in work:

        def body(i, carry, z=z, planes=planes, slope_ref=slope_ref, mixed_ref=mixed_ref, held=held):
            x = i * number
            heads = [head_ref[o] for o in range(components)]
            sides = []
            for d in range(2):
                columns = []
                place = pl.multiple_of((z + d) * GX + x, number)
                residue = r_ref[pl.ds(place, number), :]
                for j in range(number):
                    t = (held + d) * GX + x + j
                    mixed = mixed_ref[t].astype(jnp.float32)
                    total = None
                    for o in range(components):
                        row = residue[j : j + 1, o * width : (o + 1) * width]
                        term = wo_ref[o] * row
                        total = term if total is None else total + term
                        heads[o] = heads[o] + mixed * row
                    grads = total * slope_ref[t]
                    stack = [shifted(grads, -1), grads, shifted(grads, 1), rest]
                    columns.append(jnp.concatenate(stack, axis=0).astype(jnp.bfloat16))
                sides.append(jnp.concatenate(columns, axis=1))
            for o in range(components):
                head_ref[o] = heads[o]
            acc_ref[...] += lax.dot_general(
                patch_of(planes, x, number),
                jnp.concatenate(sides, axis=0),
                (((1,), (1,)), ((), ())),
                preferred_element_type=jnp.float32,
            )
            return carry

        lax.fori_loop(0, GX // number, body, 0)
    rows = grad_ref.shape[0]
    step = acc_ref.shape[0] - rows
    grad_ref[...] = acc_ref[:rows, :128] + acc_ref[step:, 128:]


def call(kernel, shapes, number, flops, scratch=()):
    return pl.pallas_call(
        kernel,
        out_shape=shapes,
        in_specs=[VMEM] * number,
        out_specs=jax.tree.map(lambda _: VMEM, shapes),
        scratch_shapes=list(scratch),
        compiler_params=pltpu.CompilerParams(vmem_limit_bytes=VMEM_BYTES),
        cost_estimate=pl.CostEstimate(
            flops=flops, bytes_accessed=1 << 23, transcendentals=1 << 20
        ),
    )


def swapped_halves(array, axis, flag):
    half = array.shape[axis] // 2
    first = lax.slice_in_dim(array, 0, half, axis=axis)
    second = lax.slice_in_dim(array, half, 2 * half, axis=axis)
    return jnp.where(flag == 0, array, jnp.concatenate([second, first], axis=axis))


def exchanged(array):
    return lax.ppermute(array, "chan", [(0, 1), (1, 0)])


def to_all(array):
    return lax.all_to_all(array, "slab", split_axis=0, concat_axis=0, tiled=True)


def per_device(
    point_features,
    kernel_blocks,
    owner_slab,
    tile_index,
    point_count,
    targets,
    w_lift,
    w_conv,
    w_out,
):
    owners = lax.axis_size("slab")
    blocks = point_features.shape[0]
    half_feat = point_features.shape[1]
    points = point_features.shape[2]
    width = kernel_blocks.shape[2]
    channels = w_lift.shape[1]
    half_chan = w_conv.shape[2]
    components = targets.shape[1]
    capacity = max(2, 2 * blocks // owners)
    slots = owners * capacity
    tiles = CZ * GX
    chan_lane = lax.axis_index("chan")
    f32, bf16 = jnp.float32, jnp.bfloat16

    w_up = swapped_halves(swapped_halves(w_lift, 0, chan_lane), 1, chan_lane).T
    w_taps = swapped_halves(w_conv, 1, chan_lane).reshape(3, 3, 3, channels, half_chan)
    w_taps = w_taps.transpose(2, 4, 0, 1, 3)
    w_pair = [jnp.pad(w_taps, ((0, 0), (0, 0), (d, 1 - d), (0, 0), (0, 0))) for d in range(2)]
    w_pair = jnp.stack(w_pair).reshape(6 * half_chan, 12 * channels)
    w_head = jnp.kron(jnp.eye(4, dtype=bf16), w_out)
    w_spread = jnp.broadcast_to(w_out.astype(f32)[:, :, None], (components, half_chan, width))

    live_mask = lax.broadcasted_iota(jnp.int32, (blocks, points), 1) < point_count[:, None]
    masked = jnp.where(live_mask[:, None, :], point_features, jnp.zeros_like(point_features))
    lifted = jnp.einsum("kfb,kbv->kfv", masked, kernel_blocks, preferred_element_type=f32)
    lifted = lifted.astype(bf16)
    target_owner = owner_slab[:, 0]
    matches = (target_owner[:, None] == jnp.arange(owners, dtype=jnp.int32)[None, :]).astype(
        jnp.int32
    )
    earlier = jnp.cumsum(matches, axis=0) - matches
    position = target_owner * capacity + jnp.sum(earlier * matches, axis=1)
    placing = position[None, :] == jnp.arange(slots, dtype=jnp.int32)[:, None]
    place_b = placing.astype(bf16)
    place_f = placing.astype(f32)
    outgoing = jnp.einsum(
        "sk,kn->sn",
        place_b,
        lifted.reshape(blocks, half_feat * width),
        preferred_element_type=f32,
    ).astype(bf16)
    tile_ids = (jnp.sum(jnp.where(placing, tile_index[None, :] + 1, 0), axis=1) - 1).astype(bf16)
    id_lanes = jnp.broadcast_to(tile_ids[:, None], (slots, 128))
    packed = jnp.concatenate([outgoing, id_lanes], axis=1)
    arrived = to_all(packed.reshape(owners, capacity, -1)).reshape(slots, -1)
    own_slots = arrived[:, : half_feat * width]
    peer_slots = exchanged(own_slots)
    arrived_ids = arrived[:, half_feat * width].astype(f32).astype(jnp.int32)
    selecting = arrived_ids[None, :] == jnp.arange(tiles, dtype=jnp.int32)[:, None]
    select_f = selecting.astype(f32)

    latent = call(
        lift_kernel,
        jax.ShapeDtypeStruct((CZ, GX + 2, channels, width), bf16),
        4,
        1 << 30,
        [pltpu.VMEM((tiles * channels, width), f32)],
    )(selecting.astype(bf16), own_slots, peer_slots, w_up)

    up = [(i, i + 1) for i in range(owners - 1)]
    down = [(j, i) for i, j in up]
    before = lax.ppermute(latent[CZ - 1 :], "slab", up)
    after = lax.ppermute(latent[:1], "slab", down)
    ends = 2 * GX
    shapes = (
        jax.ShapeDtypeStruct((tiles // 2, half_chan, width), f32),
        jax.ShapeDtypeStruct((tiles // 2, half_chan, width), bf16),
        jax.ShapeDtypeStruct((tiles // 2 * components, width), f32),
    )
    inner = call(inner_kernel, shapes, 3, 1 << 33)(latent, w_pair, w_head)
    outer = call(outer_kernel, shapes, 5, 1 << 33)(latent, before, after, w_pair, w_head)

    outer_select = jnp.concatenate([select_f[:ends], select_f[tiles - ends :]], axis=0)
    returning = jnp.einsum(
        "ts,tn->sn", select_f[ends : tiles - ends], inner[2].reshape(tiles // 2, -1), precision=HIGH
    ) + jnp.einsum("ts,tn->sn", outer_select, outer[2].reshape(tiles // 2, -1), precision=HIGH)
    received = to_all(returning.reshape(owners, capacity, -1)).reshape(slots, -1)
    per_block = jnp.einsum("sk,sn->kn", place_f, received, precision=HIGH)
    per_block = (per_block + exchanged(per_block)).reshape(blocks, components, width)
    first = lax.reduce_precision(per_block, 8, 7)
    second = lax.reduce_precision(per_block - first, 8, 7)
    third = per_block - first - second
    pieces = jnp.concatenate([first, second, third], axis=1).astype(bf16)
    terms = jnp.einsum("kqv,kbv->kqb", pieces, kernel_blocks, preferred_element_type=f32)
    terms = terms.reshape(blocks, 3, components, points)
    prediction = terms[:, 0] + (terms[:, 1] + terms[:, 2])
    error = jnp.where(live_mask[:, None, :], prediction - targets, 0.0)
    doubled = (2.0 * error).astype(bf16)
    residue = jnp.einsum("kob,kbv->kov", doubled, kernel_blocks, preferred_element_type=f32)
    sent = jnp.einsum(
        "sk,kn->sn", place_f, residue.reshape(blocks, components * width), precision=HIGH
    )
    slot_residue = to_all(sent.reshape(owners, capacity, -1)).reshape(slots, -1)
    tile_residue = jnp.einsum("ts,sn->tn", select_f, slot_residue, precision=HIGH)

    conv_terms, head_terms = call(
        grad_kernel,
        (
            jax.ShapeDtypeStruct((9 * channels, 128), f32),
            jax.ShapeDtypeStruct((components, half_chan, width), f32),
        ),
        9,
        1 << 33,
        [pltpu.VMEM((12 * channels, 256), f32)],
    )(latent, before, after, inner[0], inner[1], outer[0], outer[1], tile_residue, w_spread)
    conv_terms = conv_terms[:, : 3 * half_chan]

    squared = jnp.sum(error * error)
    point_total = jnp.sum(point_count).astype(f32)
    sizes = (conv_terms.size, components * half_chan)
    flat = jnp.concatenate(
        [
            conv_terms.reshape(-1),
            jnp.sum(head_terms, axis=2).reshape(-1),
            squared.reshape(1),
            point_total.reshape(1),
        ]
    )
    piece = -(-flat.shape[0] // (owners * 128)) * 128
    flat = jnp.pad(flat, (0, owners * piece - flat.shape[0])).reshape(owners, piece)
    share = jnp.sum(to_all(flat), axis=0)
    summed = to_all(jnp.broadcast_to(share[None], (owners, piece))).reshape(-1)
    conv_sum = summed[: sizes[0]].reshape(3, 3, channels, 3, half_chan)
    conv_sum = conv_sum.transpose(0, 1, 3, 2, 4).reshape(27, channels, half_chan)
    conv_sum = swapped_halves(conv_sum, 1, chan_lane)
    head_sum = summed[sizes[0] : sizes[0] + sizes[1]].reshape(components, half_chan)
    error_sum = summed[sizes[0] + sizes[1]]
    total_sum = summed[sizes[0] + sizes[1] + 1]
    factor = lax.rsqrt(components * total_sum)
    return (conv_sum * factor, head_sum * factor, (error_sum / (components * total_sum)).reshape(1))


def solution(mesh):
    placed = (
        P(("groups", "slab"), "chan", None),
        P(("groups", "slab"), None, None),
        P(("groups", "slab"), None),
        P(("groups", "slab")),
        P(("groups", "slab")),
        P(("groups", "slab"), None, None),
        P(),
        P(None, None, "chan"),
        P(None, "chan"),
    )
    return jax.shard_map(
        per_device,
        mesh=mesh,
        in_specs=placed,
        out_specs=(P("groups", None, "chan"), P("groups", "chan"), P("groups")),
        check_vma=False,
    )
```

```python
import functools

import jax
import jax.numpy as jnp
from jax import lax
from jax.experimental import pallas as pl
from jax.experimental.pallas import tpu as pltpu
from jax.sharding import PartitionSpec as P

GX = 32
CZ = 8


HIGH = lax.Precision.HIGHEST
VMEM_BYTES = 56 * 1024 * 1024
VMEM = pl.BlockSpec(memory_space=pltpu.VMEM)


def lift_kernel(sel_ref, own_ref, peer_ref, w_ref, out_ref, surf_ref):
    width, feats = out_ref.shape[3], w_ref.shape[1]
    tiles = sel_ref.shape[0]
    half = feats // 2
    zero = jnp.zeros(out_ref.shape[2:], out_ref.dtype)
    for z in range(out_ref.shape[0]):
        out_ref[z, 0] = zero
        out_ref[z, GX + 1] = zero
    sel = sel_ref[...]
    for side, ref in enumerate((own_ref, peer_ref)):
        for pair in range(half // 2):
            part = jnp.dot(
                sel,
                ref[:, 2 * pair * width : 2 * (pair + 1) * width],
                preferred_element_type=jnp.float32,
            )
            for j in range(2):
                feat = side * half + 2 * pair + j
                surf_ref[pl.ds(feat, tiles, stride=feats), :] = part[:, j * width : (j + 1) * width]
    w = w_ref[...]

    def body(i, carry):
        rows = surf_ref[pl.ds(pl.multiple_of(i * 2 * feats, 2 * feats), 2 * feats), :]
        rows = rows.astype(jnp.bfloat16)
        both = jnp.concatenate([rows[:feats], rows[feats:]], axis=1)
        res = jnp.dot(w, both, preferred_element_type=jnp.float32).astype(jnp.bfloat16)
        z = i // (GX // 2)
        x = (i % (GX // 2)) * 2
        out_ref[z, x + 1] = res[:, :width]
        out_ref[z, x + 2] = res[:, width:]
        return carry

    lax.fori_loop(0, tiles // 2, body, 0, unroll=4)


def shifted(array, by):
    width = array.shape[1]
    lane = lax.broadcasted_iota(jnp.int32, array.shape, 1)
    edge = 0 if by == 1 else width - 1
    return jnp.where(lane == edge, 0.0, pltpu.roll(array, by % width, 1))


def patch_of(planes, x, number):
    rows = []
    for ref, z in planes:
        for e in range(3):
            rows.append(jnp.concatenate([ref[z, x + e + j] for j in range(number)], axis=1))
    return jnp.concatenate(rows, axis=0)


def conv_pairs(pairs, w_ref, wo_ref, slope_ref, mixed_ref, p_ref):
    half, width = slope_ref.shape[1:]
    components = p_ref.shape[0] // slope_ref.shape[0]
    w = w_ref[...]
    wo = wo_ref[...]
    for number, planes in enumerate(pairs):

        def body(i, carry, number=number, planes=planes):
            x = i * 2
            res = jnp.dot(w, patch_of(planes, x, 2), preferred_element_type=jnp.float32)
            tiles = []
            for d in range(2):
                ref, z = planes[d + 1]
                for j in range(2):
                    t = (2 * number + d) * GX + x + j
                    part = res[3 * half * d : 3 * half * (d + 1), j * width : (j + 1) * width]
                    hidden = part[half : 2 * half] + (
                        shifted(part[:half], 1) + shifted(part[2 * half :], -1)
                    )
                    s = 1.0 / (1.0 + jnp.exp(-hidden))
                    own = ref[z, x + 1 + j][:half].astype(jnp.float32)
                    mixed = (own + hidden * s).astype(jnp.bfloat16)
                    slope_ref[t] = s * (1.0 + hidden * (1.0 - s))
                    mixed_ref[t] = mixed
                    tiles.append(mixed)
            heads = jnp.dot(
                wo, jnp.concatenate(tiles, axis=0), preferred_element_type=jnp.float32
            )
            rows = 2 * components
            for d in range(2):
                start = pl.multiple_of(((2 * number + d) * GX + x) * components, rows)
                p_ref[pl.ds(start, rows), :] = heads[d * rows : (d + 1) * rows]
            return carry

        lax.fori_loop(0, GX // 2, body, 0, unroll=2)


def inner_kernel(lat_ref, w_ref, wo_ref, slope_ref, mixed_ref, p_ref):
    pairs = [[(lat_ref, z + k) for k in range(-1, 3)] for z in range(2, CZ - 2, 2)]
    conv_pairs(pairs, w_ref, wo_ref, slope_ref, mixed_ref, p_ref)


def outer_kernel(lat_ref, low_ref, high_ref, w_ref, wo_ref, slope_ref, mixed_ref, p_ref):
    pairs = outer_pairs(lat_ref, low_ref, high_ref)
    conv_pairs(pairs, w_ref, wo_ref, slope_ref, mixed_ref, p_ref)


def outer_pairs(lat_ref, low_ref, high_ref):
    first = [(low_ref, 0)] + [(lat_ref, z) for z in range(3)]
    return [first, [(lat_ref, z) for z in range(CZ - 3, CZ)] + [(high_ref, 0)]]


def grad_kernel(
    lat_ref, low_ref, high_ref, inner_slope, inner_mixed, outer_slope, outer_mixed,
    r_ref, wo_ref, grad_ref, head_ref, acc_ref,
):
    width = lat_ref.shape[3]
    components, half = head_ref.shape[:2]
    number = 8
    acc_ref[...] = jnp.zeros_like(acc_ref)
    head_ref[...] = jnp.zeros_like(head_ref)
    ends = outer_pairs(lat_ref, low_ref, high_ref)
    work = [(0, ends[0], outer_slope, outer_mixed, 0)]
    for z in range(2, CZ - 2, 2):
        planes = [(lat_ref, z + k) for k in range(-1, 3)]
        work.append((z, planes, inner_slope, inner_mixed, z - 2))
    work.append((CZ - 2, ends[1], outer_slope, outer_mixed, 2))
    rest = jnp.zeros((128 - 3 * half, width), jnp.float32)
    for z, planes, slope_ref, mixed_ref, held in work:

        def body(i, carry, z=z, planes=planes, slope_ref=slope_ref, mixed_ref=mixed_ref, held=held):
            x = i * number
            heads = [head_ref[o] for o in range(components)]
            sides = []
            for d in range(2):
                columns = []
                place = pl.multiple_of((z + d) * GX + x, number)
                residue = r_ref[pl.ds(place, number), :]
                for j in range(number):
                    t = (held + d) * GX + x + j
                    mixed = mixed_ref[t].astype(jnp.float32)
                    total = None
                    for o in range(components):
                        row = residue[j : j + 1, o * width : (o + 1) * width]
                        term = wo_ref[o] * row
                        total = term if total is None else total + term
                        heads[o] = heads[o] + mixed * row
                    grads = total * slope_ref[t]
                    stack = [shifted(grads, -1), grads, shifted(grads, 1), rest]
                    columns.append(jnp.concatenate(stack, axis=0).astype(jnp.bfloat16))
                sides.append(jnp.concatenate(columns, axis=1))
            for o in range(components):
                head_ref[o] = heads[o]
            acc_ref[...] += lax.dot_general(
                patch_of(planes, x, number),
                jnp.concatenate(sides, axis=0),
                (((1,), (1,)), ((), ())),
                preferred_element_type=jnp.float32,
            )
            return carry

        lax.fori_loop(0, GX // number, body, 0)
    rows = grad_ref.shape[0]
    step = acc_ref.shape[0] - rows
    grad_ref[...] = acc_ref[:rows, :128] + acc_ref[step:, 128:]


def call(kernel, shapes, number, flops, scratch=()):
    return pl.pallas_call(
        kernel,
        out_shape=shapes,
        in_specs=[VMEM] * number,
        out_specs=jax.tree.map(lambda _: VMEM, shapes),
        scratch_shapes=list(scratch),
        compiler_params=pltpu.CompilerParams(vmem_limit_bytes=VMEM_BYTES),
        cost_estimate=pl.CostEstimate(
            flops=flops, bytes_accessed=1 << 23, transcendentals=1 << 20
        ),
    )


def swapped_halves(array, axis, flag):
    half = array.shape[axis] // 2
    first = lax.slice_in_dim(array, 0, half, axis=axis)
    second = lax.slice_in_dim(array, half, 2 * half, axis=axis)
    return jnp.where(flag == 0, array, jnp.concatenate([second, first], axis=axis))


def exchanged(array):
    return lax.ppermute(array, "chan", [(0, 1), (1, 0)])


MESH = pl.DeviceIdType.MESH


def greet_all(n, me):
    barrier = pltpu.get_barrier_semaphore()

    def greet(d, carry):
        peer = lax.rem(me + d, n)
        pl.semaphore_signal(barrier, inc=1, device_id={"slab": peer}, device_id_type=MESH)
        return carry

    lax.fori_loop(1, n, greet, 0)
    pl.semaphore_wait(barrier, n - 1)


def swap_all(n, me, source, dest_ref, send_sem, recv_sem):
    def copy(peer, place, d):
        return pltpu.make_async_remote_copy(
            src_ref=source(peer),
            dst_ref=dest_ref.at[place],
            send_sem=send_sem.at[d],
            recv_sem=recv_sem.at[d],
            device_id={"slab": peer},
            device_id_type=MESH,
        )

    def start(d, carry):
        copy(lax.rem(me + d, n), me, d).start()
        return carry

    def finish(d, carry):
        copy(lax.rem(me + d, n), me, d).wait_send()
        peer = lax.rem(me + n - d, n)
        copy(peer, peer, d).wait_recv()
        return carry

    lax.fori_loop(1, n, start, 0)
    return lambda: lax.fori_loop(1, n, finish, 0)


def all_to_all_kernel(n, in_ref, out_ref, send_sem, recv_sem):
    me = lax.axis_index("slab")
    greet_all(n, me)
    finish = swap_all(n, me, lambda peer: in_ref.at[peer], out_ref, send_sem, recv_sem)
    out_ref[me] = in_ref[me]
    finish()


def all_sum_kernel(n, in_ref, out_ref, land_ref, share_ref, send_sem, recv_sem, send2, recv2):
    me = lax.axis_index("slab")
    greet_all(n, me)
    swap_all(n, me, lambda peer: in_ref.at[peer], land_ref, send_sem, recv_sem)()
    total = lax.fori_loop(
        1, n, lambda d, total: total + land_ref[lax.rem(me + d, n)], in_ref[me]
    )
    share_ref[...] = total
    finish = swap_all(n, me, lambda peer: share_ref, out_ref, send2, recv2)
    out_ref[me] = total
    finish()


def exchange_call(kernel, array, ident, pairs, scratch=()):
    n = array.shape[0]
    return pl.pallas_call(
        functools.partial(kernel, n),
        out_shape=jax.ShapeDtypeStruct(array.shape, array.dtype),
        in_specs=[VMEM],
        out_specs=VMEM,
        scratch_shapes=list(scratch) + [pltpu.SemaphoreType.DMA((n,))] * (2 * pairs),
        compiler_params=pltpu.CompilerParams(
            collective_id=ident, has_side_effects=True, vmem_limit_bytes=VMEM_BYTES
        ),
    )(array)


def to_all(array, ident):
    if array.shape[1] % 16 == 0:
        return exchange_call(all_to_all_kernel, array, ident, 1)
    return lax.all_to_all(array, "slab", split_axis=0, concat_axis=0, tiled=True)


def summed_over_slab(array):
    scratch = [pltpu.VMEM(array.shape, array.dtype), pltpu.VMEM(array.shape[1:], array.dtype)]
    return exchange_call(all_sum_kernel, array, 3, 2, scratch)


def per_device(
    point_features,
    kernel_blocks,
    owner_slab,
    tile_index,
    point_count,
    targets,
    w_lift,
    w_conv,
    w_out,
):
    owners = lax.axis_size("slab")
    blocks = point_features.shape[0]
    half_feat = point_features.shape[1]
    points = point_features.shape[2]
    width = kernel_blocks.shape[2]
    channels = w_lift.shape[1]
    half_chan = w_conv.shape[2]
    components = targets.shape[1]
    capacity = max(2, 2 * blocks // owners)
    slots = owners * capacity
    tiles = CZ * GX
    chan_lane = lax.axis_index("chan")
    f32, bf16 = jnp.float32, jnp.bfloat16

    w_up = swapped_halves(swapped_halves(w_lift, 0, chan_lane), 1, chan_lane).T
    w_taps = swapped_halves(w_conv, 1, chan_lane).reshape(3, 3, 3, channels, half_chan)
    w_taps = w_taps.transpose(2, 4, 0, 1, 3)
    w_pair = [jnp.pad(w_taps, ((0, 0), (0, 0), (d, 1 - d), (0, 0), (0, 0))) for d in range(2)]
    w_pair = jnp.stack(w_pair).reshape(6 * half_chan, 12 * channels)
    w_head = jnp.kron(jnp.eye(4, dtype=bf16), w_out)
    w_spread = jnp.broadcast_to(w_out.astype(f32)[:, :, None], (components, half_chan, width))

    live_mask = lax.broadcasted_iota(jnp.int32, (blocks, points), 1) < point_count[:, None]
    masked = jnp.where(live_mask[:, None, :], point_features, jnp.zeros_like(point_features))
    lifted = jnp.einsum("kfb,kbv->kfv", masked, kernel_blocks, preferred_element_type=f32)
    lifted = lifted.astype(bf16)
    target_owner = owner_slab[:, 0]
    matches = (target_owner[:, None] == jnp.arange(owners, dtype=jnp.int32)[None, :]).astype(
        jnp.int32
    )
    earlier = jnp.cumsum(matches, axis=0) - matches
    position = target_owner * capacity + jnp.sum(earlier * matches, axis=1)
    placing = position[None, :] == jnp.arange(slots, dtype=jnp.int32)[:, None]
    place_b = placing.astype(bf16)
    place_f = placing.astype(f32)
    outgoing = jnp.einsum(
        "sk,kn->sn",
        place_b,
        lifted.reshape(blocks, half_feat * width),
        preferred_element_type=f32,
    ).astype(bf16)
    tile_ids = (jnp.sum(jnp.where(placing, tile_index[None, :] + 1, 0), axis=1) - 1).astype(bf16)
    id_lanes = jnp.broadcast_to(tile_ids[:, None], (slots, 128))
    packed = jnp.concatenate([outgoing, id_lanes], axis=1)
    arrived = to_all(packed.reshape(owners, capacity, -1), 0).reshape(slots, -1)
    own_slots = arrived[:, : half_feat * width]
    peer_slots = exchanged(own_slots)
    arrived_ids = arrived[:, half_feat * width].astype(f32).astype(jnp.int32)
    selecting = arrived_ids[None, :] == jnp.arange(tiles, dtype=jnp.int32)[:, None]
    select_f = selecting.astype(f32)

    latent = call(
        lift_kernel,
        jax.ShapeDtypeStruct((CZ, GX + 2, channels, width), bf16),
        4,
        1 << 30,
        [pltpu.VMEM((tiles * channels, width), f32)],
    )(selecting.astype(bf16), own_slots, peer_slots, w_up)

    up = [(i, i + 1) for i in range(owners - 1)]
    down = [(j, i) for i, j in up]
    before = lax.ppermute(latent[CZ - 1 :], "slab", up)
    after = lax.ppermute(latent[:1], "slab", down)
    ends = 2 * GX
    shapes = (
        jax.ShapeDtypeStruct((tiles // 2, half_chan, width), f32),
        jax.ShapeDtypeStruct((tiles // 2, half_chan, width), bf16),
        jax.ShapeDtypeStruct((tiles // 2 * components, width), f32),
    )
    inner = call(inner_kernel, shapes, 3, 1 << 33)(latent, w_pair, w_head)
    outer = call(outer_kernel, shapes, 5, 1 << 33)(latent, before, after, w_pair, w_head)

    outer_select = jnp.concatenate([select_f[:ends], select_f[tiles - ends :]], axis=0)
    returning = jnp.einsum(
        "ts,tn->sn", select_f[ends : tiles - ends], inner[2].reshape(tiles // 2, -1), precision=HIGH
    ) + jnp.einsum("ts,tn->sn", outer_select, outer[2].reshape(tiles // 2, -1), precision=HIGH)
    received = to_all(returning.reshape(owners, capacity, -1), 1).reshape(slots, -1)
    per_block = jnp.einsum("sk,sn->kn", place_f, received, precision=HIGH)
    per_block = (per_block + exchanged(per_block)).reshape(blocks, components, width)
    first = lax.reduce_precision(per_block, 8, 7)
    second = lax.reduce_precision(per_block - first, 8, 7)
    third = per_block - first - second
    pieces = jnp.concatenate([first, second, third], axis=1).astype(bf16)
    terms = jnp.einsum("kqv,kbv->kqb", pieces, kernel_blocks, preferred_element_type=f32)
    terms = terms.reshape(blocks, 3, components, points)
    prediction = terms[:, 0] + (terms[:, 1] + terms[:, 2])
    error = jnp.where(live_mask[:, None, :], prediction - targets, 0.0)
    doubled = (2.0 * error).astype(bf16)
    residue = jnp.einsum("kob,kbv->kov", doubled, kernel_blocks, preferred_element_type=f32)
    sent = jnp.einsum(
        "sk,kn->sn", place_f, residue.reshape(blocks, components * width), precision=HIGH
    )
    slot_residue = to_all(sent.reshape(owners, capacity, -1), 2).reshape(slots, -1)
    tile_residue = jnp.einsum("ts,sn->tn", select_f, slot_residue, precision=HIGH)

    conv_terms, head_terms = call(
        grad_kernel,
        (
            jax.ShapeDtypeStruct((9 * channels, 128), f32),
            jax.ShapeDtypeStruct((components, half_chan, width), f32),
        ),
        9,
        1 << 33,
        [pltpu.VMEM((12 * channels, 256), f32)],
    )(latent, before, after, inner[0], inner[1], outer[0], outer[1], tile_residue, w_spread)
    conv_terms = conv_terms[:, : 3 * half_chan]

    squared = jnp.sum(error * error)
    point_total = jnp.sum(point_count).astype(f32)
    sizes = (conv_terms.size, components * half_chan)
    flat = jnp.concatenate(
        [
            conv_terms.reshape(-1),
            jnp.sum(head_terms, axis=2).reshape(-1),
            squared.reshape(1),
            point_total.reshape(1),
        ]
    )
    piece = -(-flat.shape[0] // (owners * 1024)) * 1024
    flat = jnp.pad(flat, (0, owners * piece - flat.shape[0]))
    summed = summed_over_slab(flat.reshape(owners, piece // 128, 128)).reshape(-1)
    conv_sum = summed[: sizes[0]].reshape(3, 3, channels, 3, half_chan)
    conv_sum = conv_sum.transpose(0, 1, 3, 2, 4).reshape(27, channels, half_chan)
    conv_sum = swapped_halves(conv_sum, 1, chan_lane)
    head_sum = summed[sizes[0] : sizes[0] + sizes[1]].reshape(components, half_chan)
    error_sum = summed[sizes[0] + sizes[1]]
    total_sum = summed[sizes[0] + sizes[1] + 1]
    factor = lax.rsqrt(components * total_sum)
    return (conv_sum * factor, head_sum * factor, (error_sum / (components * total_sum)).reshape(1))


def solution(mesh):
    placed = (
        P(("groups", "slab"), "chan", None),
        P(("groups", "slab"), None, None),
        P(("groups", "slab"), None),
        P(("groups", "slab")),
        P(("groups", "slab")),
        P(("groups", "slab"), None, None),
        P(),
        P(None, None, "chan"),
        P(None, "chan"),
    )
    return jax.shard_map(
        per_device,
        mesh=mesh,
        in_specs=placed,
        out_specs=(P("groups", None, "chan"), P("groups", "chan"), P("groups")),
        check_vma=False,
    )
```

```python
import functools

import jax
import jax.numpy as jnp
from jax import lax
from jax.experimental import pallas as pl
from jax.experimental.pallas import tpu as pltpu
from jax.sharding import PartitionSpec as P

GX = 32
CZ = 8


HIGH = lax.Precision.HIGHEST
VMEM_BYTES = 56 * 1024 * 1024
VMEM = pl.BlockSpec(memory_space=pltpu.VMEM)


def lift_kernel(sel_ref, own_ref, peer_ref, w_ref, out_ref, surf_ref):
    width, feats = out_ref.shape[3], w_ref.shape[1]
    tiles = sel_ref.shape[0]
    half = feats // 2
    zero = jnp.zeros(out_ref.shape[2:], out_ref.dtype)
    for z in range(out_ref.shape[0]):
        out_ref[z, 0] = zero
        out_ref[z, GX + 1] = zero
    sel = sel_ref[...]
    for side, ref in enumerate((own_ref, peer_ref)):
        for pair in range(half // 2):
            part = jnp.dot(
                sel,
                ref[:, 2 * pair * width : 2 * (pair + 1) * width],
                preferred_element_type=jnp.float32,
            )
            for j in range(2):
                feat = side * half + 2 * pair + j
                surf_ref[pl.ds(feat, tiles, stride=feats), :] = part[:, j * width : (j + 1) * width]
    w = w_ref[...]

    def body(i, carry):
        rows = surf_ref[pl.ds(pl.multiple_of(i * 2 * feats, 2 * feats), 2 * feats), :]
        rows = rows.astype(jnp.bfloat16)
        both = jnp.concatenate([rows[:feats], rows[feats:]], axis=1)
        res = jnp.dot(w, both, preferred_element_type=jnp.float32).astype(jnp.bfloat16)
        z = i // (GX // 2)
        x = (i % (GX // 2)) * 2
        out_ref[z, x + 1] = res[:, :width]
        out_ref[z, x + 2] = res[:, width:]
        return carry

    lax.fori_loop(0, tiles // 2, body, 0, unroll=32)


def shifted(array, by):
    width = array.shape[1]
    lane = lax.broadcasted_iota(jnp.int32, array.shape, 1)
    edge = 0 if by == 1 else width - 1
    return jnp.where(lane == edge, 0.0, pltpu.roll(array, by % width, 1))


def patch_of(planes, x, number):
    rows = []
    for ref, z in planes:
        for e in range(3):
            rows.append(jnp.concatenate([ref[z, x + e + j] for j in range(number)], axis=1))
    return jnp.concatenate(rows, axis=0)


def conv_pairs(pairs, w_ref, wo_ref, slope_ref, mixed_ref, p_ref):
    half, width = slope_ref.shape[1:]
    components = p_ref.shape[0] // slope_ref.shape[0]
    w = w_ref[...]
    wo = wo_ref[...]
    for number, planes in enumerate(pairs):

        def body(i, carry, number=number, planes=planes):
            x = i * 2
            res = jnp.dot(w, patch_of(planes, x, 2), preferred_element_type=jnp.float32)
            tiles = []
            for d in range(2):
                ref, z = planes[d + 1]
                for j in range(2):
                    t = (2 * number + d) * GX + x + j
                    part = res[3 * half * d : 3 * half * (d + 1), j * width : (j + 1) * width]
                    hidden = part[half : 2 * half] + (
                        shifted(part[:half], 1) + shifted(part[2 * half :], -1)
                    )
                    s = 1.0 / (1.0 + jnp.exp(-hidden))
                    own = ref[z, x + 1 + j][:half].astype(jnp.float32)
                    mixed = (own + hidden * s).astype(jnp.bfloat16)
                    slope_ref[t] = s * (1.0 + hidden * (1.0 - s))
                    mixed_ref[t] = mixed
                    tiles.append(mixed)
            heads = jnp.dot(
                wo, jnp.concatenate(tiles, axis=0), preferred_element_type=jnp.float32
            )
            rows = 2 * components
            for d in range(2):
                start = pl.multiple_of(((2 * number + d) * GX + x) * components, rows)
                p_ref[pl.ds(start, rows), :] = heads[d * rows : (d + 1) * rows]
            return carry

        lax.fori_loop(0, GX // 2, body, 0, unroll=8)


def inner_kernel(lat_ref, w_ref, wo_ref, slope_ref, mixed_ref, p_ref):
    pairs = [[(lat_ref, z + k) for k in range(-1, 3)] for z in range(2, CZ - 2, 2)]
    conv_pairs(pairs, w_ref, wo_ref, slope_ref, mixed_ref, p_ref)


def outer_kernel(lat_ref, low_ref, high_ref, w_ref, wo_ref, slope_ref, mixed_ref, p_ref):
    pairs = outer_pairs(lat_ref, low_ref, high_ref)
    conv_pairs(pairs, w_ref, wo_ref, slope_ref, mixed_ref, p_ref)


def outer_pairs(lat_ref, low_ref, high_ref):
    first = [(low_ref, 0)] + [(lat_ref, z) for z in range(3)]
    return [first, [(lat_ref, z) for z in range(CZ - 3, CZ)] + [(high_ref, 0)]]


def grad_kernel(
    lat_ref, low_ref, high_ref, inner_slope, inner_mixed, outer_slope, outer_mixed,
    r_ref, wo_ref, grad_ref, head_ref, acc_ref,
):
    width = lat_ref.shape[3]
    components, half = head_ref.shape[:2]
    number = 8
    acc_ref[...] = jnp.zeros_like(acc_ref)
    head_ref[...] = jnp.zeros_like(head_ref)
    ends = outer_pairs(lat_ref, low_ref, high_ref)
    work = [(0, ends[0], outer_slope, outer_mixed, 0)]
    for z in range(2, CZ - 2, 2):
        planes = [(lat_ref, z + k) for k in range(-1, 3)]
        work.append((z, planes, inner_slope, inner_mixed, z - 2))
    work.append((CZ - 2, ends[1], outer_slope, outer_mixed, 2))
    rest = jnp.zeros((128 - 3 * half, width), jnp.float32)
    for z, planes, slope_ref, mixed_ref, held in work:

        def body(i, carry, z=z, planes=planes, slope_ref=slope_ref, mixed_ref=mixed_ref, held=held):
            x = i * number
            heads = [head_ref[o] for o in range(components)]
            sides = []
            for d in range(2):
                columns = []
                place = pl.multiple_of((z + d) * GX + x, number)
                residue = r_ref[pl.ds(place, number), :]
                for j in range(number):
                    t = (held + d) * GX + x + j
                    mixed = mixed_ref[t].astype(jnp.float32)
                    total = None
                    for o in range(components):
                        row = residue[j : j + 1, o * width : (o + 1) * width]
                        term = wo_ref[o] * row
                        total = term if total is None else total + term
                        heads[o] = heads[o] + mixed * row
                    grads = total * slope_ref[t]
                    stack = [shifted(grads, -1), grads, shifted(grads, 1), rest]
                    columns.append(jnp.concatenate(stack, axis=0).astype(jnp.bfloat16))
                sides.append(jnp.concatenate(columns, axis=1))
            for o in range(components):
                head_ref[o] = heads[o]
            acc_ref[...] += lax.dot_general(
                patch_of(planes, x, number),
                jnp.concatenate(sides, axis=0),
                (((1,), (1,)), ((), ())),
                preferred_element_type=jnp.float32,
            )
            return carry

        lax.fori_loop(0, GX // number, body, 0, unroll=2)
    rows = grad_ref.shape[0]
    step = acc_ref.shape[0] - rows
    grad_ref[...] = acc_ref[:rows, :128] + acc_ref[step:, 128:]


def call(kernel, shapes, number, flops, scratch=()):
    return pl.pallas_call(
        kernel,
        out_shape=shapes,
        in_specs=[VMEM] * number,
        out_specs=jax.tree.map(lambda _: VMEM, shapes),
        scratch_shapes=list(scratch),
        compiler_params=pltpu.CompilerParams(vmem_limit_bytes=VMEM_BYTES),
        cost_estimate=pl.CostEstimate(
            flops=flops, bytes_accessed=1 << 23, transcendentals=1 << 20
        ),
    )


def swapped_halves(array, axis, flag):
    half = array.shape[axis] // 2
    first = lax.slice_in_dim(array, 0, half, axis=axis)
    second = lax.slice_in_dim(array, half, 2 * half, axis=axis)
    return jnp.where(flag == 0, array, jnp.concatenate([second, first], axis=axis))


def exchanged(array):
    return lax.ppermute(array, "chan", [(0, 1), (1, 0)])


MESH = pl.DeviceIdType.MESH


def greet_all(n, me):
    barrier = pltpu.get_barrier_semaphore()

    def greet(d, carry):
        peer = lax.rem(me + d, n)
        pl.semaphore_signal(barrier, inc=1, device_id={"slab": peer}, device_id_type=MESH)
        return carry

    lax.fori_loop(1, n, greet, 0)
    pl.semaphore_wait(barrier, n - 1)


def swap_all(n, me, source, dest_ref, send_sem, recv_sem):
    def copy(peer, place, d):
        return pltpu.make_async_remote_copy(
            src_ref=source(peer),
            dst_ref=dest_ref.at[place],
            send_sem=send_sem.at[d],
            recv_sem=recv_sem.at[d],
            device_id={"slab": peer},
            device_id_type=MESH,
        )

    def start(d, carry):
        copy(lax.rem(me + d, n), me, d).start()
        return carry

    def finish(d, carry):
        copy(lax.rem(me + d, n), me, d).wait_send()
        peer = lax.rem(me + n - d, n)
        copy(peer, peer, d).wait_recv()
        return carry

    lax.fori_loop(1, n, start, 0)
    return lambda: lax.fori_loop(1, n, finish, 0)


def all_to_all_kernel(n, in_ref, out_ref, send_sem, recv_sem):
    me = lax.axis_index("slab")
    greet_all(n, me)
    finish = swap_all(n, me, lambda peer: in_ref.at[peer], out_ref, send_sem, recv_sem)
    out_ref[me] = in_ref[me]
    finish()


def all_sum_kernel(n, in_ref, out_ref, land_ref, share_ref, send_sem, recv_sem, send2, recv2):
    me = lax.axis_index("slab")
    greet_all(n, me)
    swap_all(n, me, lambda peer: in_ref.at[peer], land_ref, send_sem, recv_sem)()
    total = lax.fori_loop(
        1, n, lambda d, total: total + land_ref[lax.rem(me + d, n)], in_ref[me]
    )
    share_ref[...] = total
    finish = swap_all(n, me, lambda peer: share_ref, out_ref, send2, recv2)
    out_ref[me] = total
    finish()


def exchange_call(kernel, array, ident, pairs, scratch=()):
    n = array.shape[0]
    return pl.pallas_call(
        functools.partial(kernel, n),
        out_shape=jax.ShapeDtypeStruct(array.shape, array.dtype),
        in_specs=[VMEM],
        out_specs=VMEM,
        scratch_shapes=list(scratch) + [pltpu.SemaphoreType.DMA((n,))] * (2 * pairs),
        compiler_params=pltpu.CompilerParams(
            collective_id=ident, has_side_effects=True, vmem_limit_bytes=VMEM_BYTES
        ),
    )(array)


def to_all(array, ident):
    if array.shape[1] % 16 == 0:
        return exchange_call(all_to_all_kernel, array, ident, 1)
    return lax.all_to_all(array, "slab", split_axis=0, concat_axis=0, tiled=True)


def summed_over_slab(array):
    scratch = [pltpu.VMEM(array.shape, array.dtype), pltpu.VMEM(array.shape[1:], array.dtype)]
    return exchange_call(all_sum_kernel, array, 3, 2, scratch)


def per_device(
    point_features,
    kernel_blocks,
    owner_slab,
    tile_index,
    point_count,
    targets,
    w_lift,
    w_conv,
    w_out,
):
    owners = lax.axis_size("slab")
    blocks = point_features.shape[0]
    half_feat = point_features.shape[1]
    points = point_features.shape[2]
    width = kernel_blocks.shape[2]
    channels = w_lift.shape[1]
    half_chan = w_conv.shape[2]
    components = targets.shape[1]
    capacity = max(2, 2 * blocks // owners)
    slots = owners * capacity
    tiles = CZ * GX
    chan_lane = lax.axis_index("chan")
    f32, bf16 = jnp.float32, jnp.bfloat16

    w_up = swapped_halves(swapped_halves(w_lift, 0, chan_lane), 1, chan_lane).T
    w_taps = swapped_halves(w_conv, 1, chan_lane).reshape(3, 3, 3, channels, half_chan)
    w_taps = w_taps.transpose(2, 4, 0, 1, 3)
    w_pair = [jnp.pad(w_taps, ((0, 0), (0, 0), (d, 1 - d), (0, 0), (0, 0))) for d in range(2)]
    w_pair = jnp.stack(w_pair).reshape(6 * half_chan, 12 * channels)
    w_head = jnp.kron(jnp.eye(4, dtype=bf16), w_out)
    w_spread = jnp.broadcast_to(w_out.astype(f32)[:, :, None], (components, half_chan, width))

    live_mask = lax.broadcasted_iota(jnp.int32, (blocks, points), 1) < point_count[:, None]
    masked = jnp.where(live_mask[:, None, :], point_features, jnp.zeros_like(point_features))
    lifted = jnp.einsum("kfb,kbv->kfv", masked, kernel_blocks, preferred_element_type=f32)
    lifted = lifted.astype(bf16)
    target_owner = owner_slab[:, 0]
    matches = (target_owner[:, None] == jnp.arange(owners, dtype=jnp.int32)[None, :]).astype(
        jnp.int32
    )
    earlier = jnp.cumsum(matches, axis=0) - matches
    position = target_owner * capacity + jnp.sum(earlier * matches, axis=1)
    placing = position[None, :] == jnp.arange(slots, dtype=jnp.int32)[:, None]
    place_b = placing.astype(bf16)
    place_f = placing.astype(f32)
    outgoing = jnp.einsum(
        "sk,kn->sn",
        place_b,
        lifted.reshape(blocks, half_feat * width),
        preferred_element_type=f32,
    ).astype(bf16)
    tile_ids = (jnp.sum(jnp.where(placing, tile_index[None, :] + 1, 0), axis=1) - 1).astype(bf16)
    id_lanes = jnp.broadcast_to(tile_ids[:, None], (slots, 128))
    packed = jnp.concatenate([outgoing, id_lanes], axis=1)
    arrived = to_all(packed.reshape(owners, capacity, -1), 0).reshape(slots, -1)
    own_slots = arrived[:, : half_feat * width]
    peer_slots = exchanged(own_slots)
    arrived_ids = arrived[:, half_feat * width].astype(f32).astype(jnp.int32)
    selecting = arrived_ids[None, :] == jnp.arange(tiles, dtype=jnp.int32)[:, None]
    select_f = selecting.astype(f32)

    latent = call(
        lift_kernel,
        jax.ShapeDtypeStruct((CZ, GX + 2, channels, width), bf16),
        4,
        1 << 30,
        [pltpu.VMEM((tiles * channels, width), f32)],
    )(selecting.astype(bf16), own_slots, peer_slots, w_up)

    up = [(i, i + 1) for i in range(owners - 1)]
    down = [(j, i) for i, j in up]
    before = lax.ppermute(latent[CZ - 1 :], "slab", up)
    after = lax.ppermute(latent[:1], "slab", down)
    ends = 2 * GX
    shapes = (
        jax.ShapeDtypeStruct((tiles // 2, half_chan, width), f32),
        jax.ShapeDtypeStruct((tiles // 2, half_chan, width), bf16),
        jax.ShapeDtypeStruct((tiles // 2 * components, width), f32),
    )
    inner = call(inner_kernel, shapes, 3, 1 << 33)(latent, w_pair, w_head)
    outer = call(outer_kernel, shapes, 5, 1 << 33)(latent, before, after, w_pair, w_head)

    outer_select = jnp.concatenate([select_f[:ends], select_f[tiles - ends :]], axis=0)
    returning = jnp.einsum(
        "ts,tn->sn", select_f[ends : tiles - ends], inner[2].reshape(tiles // 2, -1), precision=HIGH
    ) + jnp.einsum("ts,tn->sn", outer_select, outer[2].reshape(tiles // 2, -1), precision=HIGH)
    received = to_all(returning.reshape(owners, capacity, -1), 1).reshape(slots, -1)
    per_block = jnp.einsum("sk,sn->kn", place_f, received, precision=HIGH)
    per_block = (per_block + exchanged(per_block)).reshape(blocks, components, width)
    first = lax.reduce_precision(per_block, 8, 7)
    second = lax.reduce_precision(per_block - first, 8, 7)
    third = per_block - first - second
    pieces = jnp.concatenate([first, second, third], axis=1).astype(bf16)
    terms = jnp.einsum("kqv,kbv->kqb", pieces, kernel_blocks, preferred_element_type=f32)
    terms = terms.reshape(blocks, 3, components, points)
    prediction = terms[:, 0] + (terms[:, 1] + terms[:, 2])
    error = jnp.where(live_mask[:, None, :], prediction - targets, 0.0)
    doubled = (2.0 * error).astype(bf16)
    residue = jnp.einsum("kob,kbv->kov", doubled, kernel_blocks, preferred_element_type=f32)
    sent = jnp.einsum(
        "sk,kn->sn", place_f, residue.reshape(blocks, components * width), precision=HIGH
    )
    slot_residue = to_all(sent.reshape(owners, capacity, -1), 2).reshape(slots, -1)
    tile_residue = jnp.einsum("ts,sn->tn", select_f, slot_residue, precision=HIGH)

    conv_terms, head_terms = call(
        grad_kernel,
        (
            jax.ShapeDtypeStruct((9 * channels, 128), f32),
            jax.ShapeDtypeStruct((components, half_chan, width), f32),
        ),
        9,
        1 << 33,
        [pltpu.VMEM((12 * channels, 256), f32)],
    )(latent, before, after, inner[0], inner[1], outer[0], outer[1], tile_residue, w_spread)
    conv_terms = conv_terms[:, : 3 * half_chan]

    squared = jnp.sum(error * error)
    point_total = jnp.sum(point_count).astype(f32)
    sizes = (conv_terms.size, components * half_chan)
    flat = jnp.concatenate(
        [
            conv_terms.reshape(-1),
            jnp.sum(head_terms, axis=2).reshape(-1),
            squared.reshape(1),
            point_total.reshape(1),
        ]
    )
    piece = -(-flat.shape[0] // (owners * 1024)) * 1024
    flat = jnp.pad(flat, (0, owners * piece - flat.shape[0]))
    summed = summed_over_slab(flat.reshape(owners, piece // 128, 128)).reshape(-1)
    conv_sum = summed[: sizes[0]].reshape(3, 3, channels, 3, half_chan)
    conv_sum = conv_sum.transpose(0, 1, 3, 2, 4).reshape(27, channels, half_chan)
    conv_sum = swapped_halves(conv_sum, 1, chan_lane)
    head_sum = summed[sizes[0] : sizes[0] + sizes[1]].reshape(components, half_chan)
    error_sum = summed[sizes[0] + sizes[1]]
    total_sum = summed[sizes[0] + sizes[1] + 1]
    factor = lax.rsqrt(components * total_sum)
    return (conv_sum * factor, head_sum * factor, (error_sum / (components * total_sum)).reshape(1))


def solution(mesh):
    placed = (
        P(("groups", "slab"), "chan", None),
        P(("groups", "slab"), None, None),
        P(("groups", "slab"), None),
        P(("groups", "slab")),
        P(("groups", "slab")),
        P(("groups", "slab"), None, None),
        P(),
        P(None, None, "chan"),
        P(None, "chan"),
    )
    return jax.shard_map(
        per_device,
        mesh=mesh,
        in_specs=placed,
        out_specs=(P("groups", None, "chan"), P("groups", "chan"), P("groups")),
        check_vma=False,
    )
```
